512 devices in a mesh: layer: 8 (over z), tile: 64 (over x, y, core).
Axes of the slice: x: 4, y: 8, z: 8, core: 2. Of those that a mesh axis runs over, the one named last changes fastest.
Arguments:
- incident: bfloat16 [2, 32768, 128], P(None, 'tile'), may hold values from -6 to 6
- sources: bfloat16 [8, 2, 32768, 128], P('layer', None, 'tile'), may hold values from -6 to 6
- green_tiles: bfloat16 [8, 768, 2, 256, 256], P('layer', 'tile'), may hold values from -0.09375 to 0.09375
- tile_rows: int32 [8, 768], P('layer', 'tile'), may hold values from 0 to 127, as said below
- tile_cols: int32 [8, 768], P('layer', 'tile'), may hold values from 0 to 1, as said below
- tile_count: int32 [8, 64], P('layer', 'tile'), may hold values from 1 to 12, 576 in all within a row
Outputs:
- traces: bfloat16 [8, 2, 32768, 128], P('layer', None, 'tile')
The draws below stay inside these ranges and needn't reach their ends.
Inputs may be any that keep to these rules, and one draw needn't show every extreme that they name: `tile_rows`: slot i of a layer belongs to tile device d = i // 12; its row block lies among the row blocks held by devices d - 1, d and d + 1, where row block r is held by device r // 2; in every layer some live slot writes to the first row block of the device on its left and some to the last of the device on its right. `tile_cols`: the column block is counted among the 2 row blocks held by the slot's own device. `tile_count`: A device's live slots are its first ones; each layer group has 9 * 64 live slots in all.
All inputs are finite; a program needn't handle non-finite values.
Results may differ from the reference program's by a relative error of at most 0.0095.
Values may be sent and summed in bfloat16 or wider, within the bound.
A program may use at most 64 MiB of HBM per device.

```python
import math
import jax
import jax.numpy as jnp
import numpy as np
from jax import lax

NI = 32768
TB = 256
TILES_DEV = 12
SRC = 64
FRONTS = 2
LAYERS = 8
BLK_DEV = 2
N_TILE = 64


def slot_pairs(key):
    nblock = NI // TB
    blocks_dev = nblock // N_TILE
    slot_total = N_TILE * TILES_DEV
    choices_all = 3 * blocks_dev * blocks_dev
    inner = jax.random.fold_in(key, 4711)
    keys = jax.random.split(inner, LAYERS * N_TILE)
    orders = jax.vmap(lambda kk: jax.random.permutation(kk, choices_all))(keys)
    picked = orders[:, :TILES_DEV].astype(jnp.int32).reshape(LAYERS, slot_total)
    slots = jnp.arange(slot_total, dtype=jnp.int32)
    owner = slots // TILES_DEV
    window_row = picked // blocks_dev
    columns = picked % blocks_dev
    rows = (owner[None, :] - 1) * blocks_dev + window_row
    rows = jnp.where(rows < 0, rows + blocks_dev, rows)
    rows = jnp.where(rows >= nblock, rows - blocks_dev, rows)
    rows = jnp.where(slots[None, :] == TILES_DEV, 0, rows)
    rows = jnp.where(slots[None, :] == (N_TILE - 2) * TILES_DEV, nblock - 1, rows)
    return (rows.astype(jnp.int32), columns.astype(jnp.int32))


def draw_tile_rows(key, part):
    rows, columns = slot_pairs(key)
    return rows


def draw_tile_cols(key, part):
    rows, columns = slot_pairs(key)
    return columns


def shard_levels(stream_key, dims, cuts, smallest, top_value):
    loudness, own = 1.0, jax.random.fold_in(stream_key, 6)
    for dim, parts in cuts:
        steps = jnp.exp(jax.random.uniform(jax.random.fold_in(own, dim), (parts,), jnp.float32, smallest / len(cuts), top_value / len(cuts)))
        loudness = loudness * jnp.repeat(steps, dims[dim] // parts).reshape([-1 if axis == dim else 1 for axis in range(len(dims))])
    return loudness


def profile(amount, total, bound, lean):
    weights = [(1 << 20) // math.isqrt(standing ** lean) + 1 for standing in range(2, amount + 1)]
    rest, given = total - bound - (amount - 1), [1] * (amount - 1)
    while rest > 0:
        free = [i for i in range(amount - 1) if given[i] < bound]
        whole, left = sum([weights[i] for i in free]), rest
        for i in free:
            addition = min(bound - given[i], max(1, left * weights[i] // whole), rest)
            given[i] = given[i] + addition
            rest = rest - addition
    return np.array([bound] + given)


def uneven(own_key, count, total, limit, skew):
    if count == 2:
        one = jax.random.randint(own_key, (), max(1, total - limit), min(limit, total - 1) + 1)
        return jnp.stack([one, total - one])
    lengths = jnp.asarray(profile(count, total, limit, skew), jnp.int32)
    couples = (count - 1) // 2
    source_of, receiver = lengths[1:1 + 2 * couples:2], lengths[2:2 + 2 * couples:2]
    room = jnp.minimum(source_of - 1, limit - receiver)
    passed = jax.random.randint(jax.random.fold_in(own_key, 1), (couples,), 0, 1 << 20) % (room + 1)
    lengths = lengths.at[1:1 + 2 * couples:2].set(source_of - passed).at[2:2 + 2 * couples:2].set(receiver + passed)
    return lengths[jax.random.permutation(jax.random.fold_in(own_key, 2), count)]


def normal_values(own_key, extent, deviation, limit, cuts=(), kind=jnp.bfloat16):
    drawn = jax.random.normal(own_key, extent, jnp.float32) * deviation
    if len(cuts) > 0:
        drawn = shard_levels(own_key, extent, cuts, -0.22, 0.18) * drawn
    return jnp.clip(drawn, min=-limit, max=limit).astype(kind)


def setup_inputs(seed: int = 0) -> dict:
    splits = jax.random.split(jax.random.key(seed), 7)
    return {
        "incident": normal_values(splits[0], (FRONTS, NI, 2 * SRC), 1.0, 6.0, ((1, 64),)),
        "sources": normal_values(splits[1], (LAYERS, FRONTS, NI, 2 * SRC), 1.0, 6.0, ((0, 8), (2, 64))),
        "green_tiles": normal_values(splits[2], (LAYERS, N_TILE * TILES_DEV, 2, TB, TB), (36 * TB // BLK_DEV) ** -0.5, 0.09375, ((0, 8), (1, 64))),
        "tile_rows": draw_tile_rows(jax.random.fold_in(splits[6], 71), 0),
        "tile_cols": draw_tile_cols(jax.random.fold_in(splits[6], 71), 0),
        "tile_count": jax.vmap(lambda own: uneven(own, N_TILE, 9 * N_TILE, TILES_DEV, 2))(jax.random.split(splits[5], LAYERS)).reshape((LAYERS, N_TILE)).astype(jnp.int32),
    }


def reference(incident, sources, green_tiles, tile_rows, tile_cols, tile_count):
    nblock = NI // TB
    blocks_dev = nblock // N_TILE
    slot_total = N_TILE * TILES_DEV
    owner = jnp.arange(slot_total, dtype=jnp.int32) // TILES_DEV
    within = jnp.arange(slot_total, dtype=jnp.int32) % TILES_DEV
    width = 2 * SRC
    trace = incident
    results = []
    for layer_index in range(LAYERS):
        blocks = trace.astype(jnp.float32).reshape(FRONTS, nblock, TB, width)
        column = (owner * blocks_dev + tile_cols[layer_index]).astype(jnp.int32)
        picked = blocks[:, column]
        swapped = jnp.concatenate([-picked[..., SRC:], picked[..., :SRC]], axis=-1)
        stacked = jnp.stack([picked, swapped], axis=2)
        tiles = green_tiles[layer_index].astype(jnp.float32)
        terms = jnp.einsum("tcab,ftcbs->ftas", tiles, stacked, precision=lax.Precision.HIGHEST)
        active = within < tile_count[layer_index][owner]
        terms = terms * active.astype(jnp.float32)[None, :, None, None]
        row_block = tile_rows[layer_index].astype(jnp.int32)
        offset = row_block // blocks_dev - owner
        total = jnp.zeros((FRONTS, nblock, TB, width), jnp.float32)
        own_terms = jnp.where((offset == 0)[None, :, None, None], terms, jnp.float32(0.0))
        total = total.at[:, row_block].add(own_terms)
        for side in (-1, 1):
            chosen = jnp.where((offset == side)[None, :, None, None], terms, jnp.float32(0.0))
            partial_sum = jnp.zeros((FRONTS, nblock, TB, width), jnp.float32).at[:, row_block].add(chosen)
            rounded = lax.optimization_barrier(partial_sum.astype(jnp.bfloat16))
            total = total + rounded.astype(jnp.float32)
        total = total.reshape(FRONTS, NI, width) + sources[layer_index].astype(jnp.float32)
        trace = total.astype(jnp.bfloat16)
        results.append(trace)
    return jnp.stack(results)
```

```python
import functools

import jax
import jax.numpy as jnp
from jax import lax
from jax.experimental import pallas as pl
from jax.experimental.pallas import tpu as pltpu
from jax.sharding import PartitionSpec as P

MESH = pl.DeviceIdType.MESH
VMEM = pl.BlockSpec(memory_space=pltpu.VMEM)
SMEM = pl.BlockSpec(memory_space=pltpu.SMEM)
ANY = pl.BlockSpec(memory_space=pl.ANY)
CHUNKS = 16
LAG = 3
F32 = jnp.float32
BF16 = jnp.bfloat16


def beside(place):
    odd = lax.rem(place, 2)
    return place - 1 + 2 * odd, place + 1 - 2 * odd


def prepare(rows_ref, cols_ref, count_ref, tiles_ref, incident_ref, source_ref,
            dense_ref, opening_ref, given_ref, held, extra, total, sem, extra_sem):
    slots, block = tiles_ref.shape[1], tiles_ref.shape[3]
    place = lax.axis_index("tile")
    across, partner = beside(place)
    live = count_ref[0, 0]
    pairs = []
    for part, owner in enumerate((across, partner, place)):
        for r in range(2):
            for c in range(2):
                wanted = owner * 2 + r
                number, first = jnp.int32(0), jnp.int32(0)
                for i in reversed(range(slots)):
                    match = (i < live) & (rows_ref[0, i] == wanted) & (cols_ref[0, i] == c)
                    number = number + match.astype(jnp.int32)
                    first = jnp.where(match, i, first)
                p = len(pairs)
                pltpu.make_async_copy(tiles_ref.at[0, first], held.at[p], sem.at[p]).start()
                pairs.append((part * 2 * block + r * block, c * block, wanted, c, number))
    chunks, width, _ = opening_ref.shape
    each, half = chunks // 2, width // 2
    for array, out in ((incident_ref, opening_ref), (source_ref.at[0], given_ref)):
        for f in range(2):
            turned = array[f].astype(F32).T
            mid = turned.shape[0] // 2
            for j in range(each):
                piece = jnp.concatenate(
                    [turned[j * half:(j + 1) * half], turned[mid + j * half:mid + (j + 1) * half]], axis=0)
                out[f * each + j] = piece.astype(BF16)
    depth = 2 * block
    for p, (at, under, wanted, c, number) in enumerate(pairs):
        pltpu.make_async_copy(tiles_ref.at[0, 0], held.at[p], sem.at[p]).wait()

        @pl.when(number == 0)
        def _():
            for s in range(2):
                dense_ref[s * depth + under:s * depth + under + block, at:at + block] = jnp.zeros((block, block), BF16)

        @pl.when(number == 1)
        def _():
            for s in range(2):
                dense_ref[s * depth + under:s * depth + under + block, at:at + block] = held[p, s].T

        @pl.when(number > 1)
        def _():
            total[...] = jnp.zeros_like(total)

            def add(i, _):
                @pl.when((i < live) & (rows_ref[0, i] == wanted) & (cols_ref[0, i] == c))
                def _():
                    copy = pltpu.make_async_copy(tiles_ref.at[0, i], extra, extra_sem)
                    copy.start()
                    copy.wait()
                    total[...] += extra[...].astype(F32)
                return 0

            lax.fori_loop(0, slots, add, 0)
            for s in range(2):
                dense_ref[s * depth + under:s * depth + under + block, at:at + block] = total[s].T.astype(BF16)


def sweep(layers, places, dense_ref, opening_ref, given_ref, out_ref,
          own_in, ext_in, side_in, mate_in, own_out, ext_out, mate_out, kept,
          own_s, ext_s, side_s, mate_s, own_r, ext_r, side_r, mate_r):
    chunks, width, rows = opening_ref.shape
    half = width // 2
    layer, place = lax.axis_index("layer"), lax.axis_index("tile")
    across, partner = beside(place)
    has = (across >= 0) & (across < places)
    above, below = layer > 0, layer < layers - 1
    barrier = pltpu.get_barrier_semaphore()

    def hello(l, t):
        pl.semaphore_signal(barrier, inc=1, device_id=(l, t), device_id_type=MESH)

    hello(layer, partner)

    @pl.when(has)
    def _():
        hello(layer, across)

    @pl.when(above)
    def _():
        hello(layer - 1, place)

    @pl.when(above & has)
    def _():
        hello(layer - 1, across)

    @pl.when(jnp.logical_not(above))
    def _():
        own_in[...] = opening_ref[...]

    @pl.when(jnp.logical_not(above & has))
    def _():
        ext_in[...] = jnp.zeros_like(ext_in)

    @pl.when(jnp.logical_not(has))
    def _():
        side_in[...] = jnp.zeros_like(side_in)

    beyond = has.astype(jnp.int32)
    pl.semaphore_wait(barrier, (1 + beyond) * (1 + below.astype(jnp.int32)))

    def send(src, dst, s, r, c, l, t):
        return pltpu.make_async_remote_copy(
            src_ref=src.at[c], dst_ref=dst.at[c], send_sem=s.at[c], recv_sem=r.at[c],
            device_id=(l, t), device_id_type=MESH)

    def to_mate(c):
        return send(mate_out, mate_in, mate_s, mate_r, c, layer, partner)

    def to_side(c):
        return send(ext_out, side_in, side_s, side_r, c, layer, across)

    def to_own(c):
        return send(own_out, own_in, own_s, own_r, c, layer + 1, place)

    def to_ext(c):
        return send(ext_out, ext_in, ext_s, ext_r, c, layer + 1, across)

    def multiply(c):
        @pl.when(above)
        def _():
            to_own(c).wait_recv()

        @pl.when(above & has)
        def _():
            to_ext(c).wait_recv()

        u = (own_in[c].astype(F32) + ext_in[c].astype(F32)).astype(BF16).astype(F32)
        turned = jnp.concatenate([-u[half:], u[:half]], axis=0)
        stacked = jnp.concatenate([u, turned], axis=1).astype(BF16)

        def part(k):
            return jnp.dot(stacked, dense_ref[:, k * rows:(k + 1) * rows], preferred_element_type=F32)

        ext_out[c] = part(0).astype(BF16)

        @pl.when(below & has)
        def _():
            to_ext(c).start()

        @pl.when(has)
        def _():
            to_side(c).start()

        mate_out[c] = part(1).astype(BF16)
        to_mate(c).start()
        kept[c] = part(2) + given_ref[c].astype(F32)

    def combine(c):
        to_mate(c).wait_recv()
        y = kept[c] + mate_in[c].astype(F32)
        kept[c] = y
        own_out[c] = y.astype(BF16)

        @pl.when(below)
        def _():
            to_own(c).start()

    def finish(c):
        @pl.when(has)
        def _():
            to_side(c).wait_recv()

        out_ref[c] = (kept[c] + side_in[c].astype(F32)).astype(BF16)

    def step(t, _):
        @pl.when(t < chunks)
        def _():
            multiply(t)

        @pl.when((t >= 1) & (t < chunks + 1))
        def _():
            combine(t - 1)

        @pl.when(t >= LAG)
        def _():
            finish(t - LAG)
        return 0

    lax.fori_loop(0, chunks + LAG, step, 0)

    def drain(c, _):
        to_mate(c).wait_send()

        @pl.when(has)
        def _():
            to_side(c).wait_send()

        @pl.when(below)
        def _():
            to_own(c).wait_send()

        @pl.when(below & has)
        def _():
            to_ext(c).wait_send()
        return 0

    lax.fori_loop(0, chunks, drain, 0)


def restore(trace_ref, out_ref, scratch):
    chunks, width, _ = trace_ref.shape
    each, half = chunks // 2, width // 2
    mid = scratch.shape[1] // 2
    for f in range(2):
        for j in range(each):
            piece = trace_ref[f * each + j].astype(F32)
            scratch[f, j * half:(j + 1) * half] = piece[:half]
            scratch[f, mid + j * half:mid + (j + 1) * half] = piece[half:]
        out_ref[0, f] = scratch[f].T.astype(BF16)


def shards(layers, places, incident, sources, green_tiles, tile_rows, tile_cols, tile_count):
    fronts, rows, columns = incident.shape
    slots, _, block, _ = green_tiles.shape[1:]
    width = fronts * columns // CHUNKS
    chunked = jax.ShapeDtypeStruct((CHUNKS, width, rows), BF16)
    dense, opening, given = pl.pallas_call(
        prepare,
        out_shape=(jax.ShapeDtypeStruct((4 * block, 3 * rows), BF16), chunked, chunked),
        in_specs=[SMEM, SMEM, SMEM, ANY, VMEM, VMEM],
        out_specs=(VMEM, VMEM, VMEM),
        scratch_shapes=[
            pltpu.VMEM((12, 2, block, block), BF16),
            pltpu.VMEM((2, block, block), BF16),
            pltpu.VMEM((2, block, block), F32),
            pltpu.SemaphoreType.DMA((12,)),
            pltpu.SemaphoreType.DMA,
        ],
        compiler_params=pltpu.CompilerParams(vmem_limit_bytes=24 * 2**20),
    )(tile_rows, tile_cols, tile_count, green_tiles, incident, sources)
    buffer = pltpu.VMEM((CHUNKS, width, rows), BF16)
    trace = pl.pallas_call(
        functools.partial(sweep, layers, places),
        out_shape=chunked,
        in_specs=[VMEM, VMEM, VMEM],
        out_specs=VMEM,
        scratch_shapes=[buffer] * 7
        + [pltpu.VMEM((CHUNKS, width, rows), F32)]
        + [pltpu.SemaphoreType.DMA((CHUNKS,))] * 8,
        compiler_params=pltpu.CompilerParams(
            collective_id=0, has_side_effects=True, vmem_limit_bytes=24 * 2**20),
    )(dense, opening, given)
    return pl.pallas_call(
        restore,
        out_shape=jax.ShapeDtypeStruct((1, fronts, rows, columns), BF16),
        in_specs=[VMEM],
        out_specs=VMEM,
        scratch_shapes=[pltpu.VMEM((fronts, columns, rows), F32)],
    )(trace)


def solution(mesh):
    return jax.shard_map(
        functools.partial(shards, mesh.shape["layer"], mesh.shape["tile"]),
        mesh=mesh,
        in_specs=(
            P(None, "tile", None),
            P("layer", None, "tile", None),
            P("layer", "tile", None, None, None),
            P("layer", "tile"),
            P("layer", "tile"),
            P("layer", "tile"),
        ),
        out_specs=P("layer", None, "tile", None),
        check_vma=False,
    )
```

```python
import functools

import jax
import jax.numpy as jnp
from jax import lax
from jax.experimental import pallas as pl
from jax.experimental.pallas import tpu as pltpu
from jax.sharding import PartitionSpec as P

MESH = pl.DeviceIdType.MESH
VMEM = pl.BlockSpec(memory_space=pltpu.VMEM)
HBM = pl.BlockSpec(memory_space=pltpu.HBM)
CHUNKS = 16
LAG = 6
F32 = jnp.float32
BF16 = jnp.bfloat16


def sweep(layers, places, rows_hbm, cols_hbm, count_hbm, tiles_hbm, incident_hbm, source_hbm, out_ref,
          rows_ref, cols_ref, count_ref, tiles_ref, incident_ref, source_ref, dense, given, result,
          own_in, ext_in, side_in, mate_in, own_out, ext_out, mate_out, kept,
          index_sem, array_sem, tile_sem,
          own_s, ext_s, side_s, mate_s, own_r, ext_r, side_r, mate_r):
    slots, block = tiles_ref.shape[0], tiles_ref.shape[2]
    chunks, width, rows = own_in.shape
    each, half = chunks // 2, width // 2
    layer, place = lax.axis_index("layer"), lax.axis_index("tile")
    odd = lax.rem(place, 2)
    partner = place + 1 - 2 * odd
    beyond = place - 1 + 2 * odd
    inner = (beyond >= 0) & (beyond < places)
    across = jnp.where(inner, beyond, partner)
    aside = jnp.where(inner, 0, chunks)
    beside_edge = (partner == 0) | (partner == places - 1)
    above, below = layer > 0, layer < layers - 1

    index_copies = [
        pltpu.make_async_copy(src, dst, index_sem.at[i])
        for i, (src, dst) in enumerate(((rows_hbm, rows_ref), (cols_hbm, cols_ref), (count_hbm, count_ref)))
    ]
    array_copies = [
        pltpu.make_async_copy(incident_hbm, incident_ref, array_sem.at[0]),
        pltpu.make_async_copy(source_hbm.at[0], source_ref, array_sem.at[1]),
    ]
    tile_copies = [pltpu.make_async_copy(tiles_hbm.at[0, i], tiles_ref.at[i], tile_sem.at[i]) for i in range(slots)]
    for copy in index_copies + array_copies[:1] + tile_copies + array_copies[1:]:
        copy.start()

    barrier = pltpu.get_barrier_semaphore()

    def hello(l, t):
        pl.semaphore_signal(barrier, inc=1, device_id=(l, t), device_id_type=MESH)

    hello(layer, partner)

    @pl.when(inner)
    def _():
        hello(layer, across)

    @pl.when(above)
    def _():
        hello(layer - 1, place)

    @pl.when(above & inner)
    def _():
        hello(layer - 1, across)

    @pl.when(above & beside_edge)
    def _():
        hello(layer - 1, partner)

    dense[slots] = jnp.zeros(dense.shape[1:], BF16)

    for copy in index_copies:
        copy.wait()
    live = count_ref[0, 0]
    keys = []
    for i in range(slots):
        row = rows_ref[0, i]
        owner = row // 2
        part = jnp.where(owner == beyond, 0, jnp.where(owner == partner, 1, 2))
        keys.append(jnp.where(i < live, part * 4 + (row - 2 * owner) * 2 + cols_ref[0, i], 16 + i))
    before = []
    for i in range(slots):
        found = jnp.int32(slots)
        for j in range(i):
            found = jnp.where(keys[j] == keys[i], j, found)
        before.append(found)
    last = []
    for p in range(12):
        found = jnp.int32(slots)
        for i in range(slots):
            found = jnp.where(keys[i] == p, i, found)
        last.append(found)

    array_copies[0].wait()

    @pl.when(jnp.logical_not(above))
    def _():
        for f in range(2):
            turned = incident_ref[f].astype(F32).T.reshape(2, each, half, rows)
            for j in range(each):
                own_in[f * each + j] = turned[:, j].reshape(width, rows).astype(BF16)

    @pl.when(jnp.logical_not(above & inner))
    def _():
        ext_in[:chunks] = jnp.zeros((chunks, width, rows), BF16)

    @pl.when(jnp.logical_not(inner))
    def _():
        side_in[:chunks] = jnp.zeros((chunks, width, rows), BF16)

    for i in range(slots):
        tile_copies[i].wait()
        for s in range(2):
            dense[i, s] = (tiles_ref[i, s].T.astype(F32) + dense[before[i], s].astype(F32)).astype(BF16)

    array_copies[1].wait()
    for f in range(2):
        given[f] = source_ref[f].astype(F32).T.reshape(2, each, half, rows)

    pl.semaphore_wait(barrier, 1 + inner.astype(jnp.int32) + 2 * below.astype(jnp.int32))

    def send(src, dst, s, r, c, l, t, to=0):
        return pltpu.make_async_remote_copy(
            src_ref=src.at[c], dst_ref=dst.at[c + to], send_sem=s.at[c], recv_sem=r.at[c + to],
            device_id=(l, t), device_id_type=MESH)

    def to_mate(c):
        return send(mate_out, mate_in, mate_s, mate_r, c, layer, partner)

    def to_side(c):
        return send(ext_out, side_in, side_s, side_r, c, layer, across, aside)

    def to_own(c):
        return send(own_out, own_in, own_s, own_r, c, layer + 1, place)

    def to_ext(c):
        return send(ext_out, ext_in, ext_s, ext_r, c, layer + 1, across, aside)

    def arrived(dst, s, r, c):
        send(dst, dst, s, r, c, layer, partner).wait_recv()

    def multiply(c, onward):
        @pl.when(above)
        def _():
            to_own(c).wait_recv()

        @pl.when(above & inner)
        def _():
            arrived(ext_in, ext_s, ext_r, c)

        u = (own_in[c].astype(F32) + ext_in[c].astype(F32)).astype(BF16).astype(F32)
        sides = (u.astype(BF16), jnp.concatenate([-u[half:], u[:half]], axis=0).astype(BF16))

        def part(k):
            outs = []
            for r in range(2):
                total = None
                for b in range(2):
                    for s in range(2):
                        term = jnp.dot(sides[s][:, b * block:(b + 1) * block],
                                       dense[last[4 * k + 2 * r + b], s], preferred_element_type=F32)
                        total = term if total is None else total + term
                outs.append(total)
            return jnp.concatenate(outs, axis=1)

        ext_out[c] = part(0).astype(BF16)
        if onward:
            to_ext(c).start()
        mate_out[c] = part(1).astype(BF16)
        to_mate(c).start()
        to_side(c).start()
        source = given[c // each, :, c % each].reshape(width, rows)
        kept[c] = part(2) + source

    def combine(c, onward):
        to_mate(c).wait_recv()
        y = kept[c] + mate_in[c].astype(F32)
        kept[c] = y
        if onward:
            own_out[c] = y.astype(BF16)
            to_own(c).start()

    def finish(c):
        @pl.when(inner)
        def _():
            arrived(side_in, side_s, side_r, c)

        result[c // each, :, c % each] = (kept[c] + side_in[c].astype(F32)).reshape(2, half, rows)

    def pipeline(onward):
        multiply(0, onward)

        def step(t, _):
            multiply(t, onward)
            combine(t - 1, onward)

            @pl.when(t >= LAG)
            def _():
                finish(t - LAG)
            return 0

        lax.fori_loop(1, chunks, step, 0)
        combine(chunks - 1, onward)

    @pl.when(below)
    def _():
        pipeline(True)

    @pl.when(jnp.logical_not(below))
    def _():
        pipeline(False)

    def leave(f):
        out_ref[0, f] = result[f].reshape(2 * each * half, rows).T.astype(BF16)

    leave(0)

    def last_step(c, _):
        finish(c)
        return 0

    lax.fori_loop(chunks - LAG, chunks, last_step, 0)
    leave(1)

    def drain(c, _):
        to_mate(c).wait_send()
        to_side(c).wait_send()

        @pl.when(below)
        def _():
            to_own(c).wait_send()
            to_ext(c).wait_send()

        @pl.when(beside_edge)
        def _():
            arrived(side_in, side_s, side_r, chunks + c)

        @pl.when(above & beside_edge)
        def _():
            arrived(ext_in, ext_s, ext_r, chunks + c)
        return 0

    lax.fori_loop(0, chunks, drain, 0)


def shards(layers, places, incident, sources, green_tiles, tile_rows, tile_cols, tile_count):
    fronts, rows, columns = incident.shape
    slots, _, block, _ = green_tiles.shape[1:]
    width = fronts * columns // CHUNKS
    buffer = pltpu.VMEM((CHUNKS, width, rows), BF16)
    double = pltpu.VMEM((2 * CHUNKS, width, rows), BF16)
    split = pltpu.VMEM((fronts, 2, CHUNKS // 2, width // 2, rows), F32)
    return pl.pallas_call(
        functools.partial(sweep, layers, places),
        out_shape=jax.ShapeDtypeStruct((1, fronts, rows, columns), BF16),
        in_specs=[HBM] * 6,
        out_specs=VMEM,
        scratch_shapes=[
            pltpu.SMEM(tile_rows.shape, jnp.int32),
            pltpu.SMEM(tile_cols.shape, jnp.int32),
            pltpu.SMEM(tile_count.shape, jnp.int32),
            pltpu.VMEM((slots, 2, block, block), BF16),
            pltpu.VMEM((fronts, rows, columns), BF16),
            pltpu.VMEM((fronts, rows, columns), BF16),
            pltpu.VMEM((slots + 1, 2, block, block), BF16),
            split,
            split,
        ]
        + [buffer, double, double] + [buffer] * 4
        + [pltpu.VMEM((CHUNKS, width, rows), F32)]
        + [pltpu.SemaphoreType.DMA((3,)), pltpu.SemaphoreType.DMA((2,)), pltpu.SemaphoreType.DMA((slots,))]
        + [pltpu.SemaphoreType.DMA((CHUNKS,))] * 4
        + [pltpu.SemaphoreType.DMA((2 * CHUNKS,))] * 4,
        compiler_params=pltpu.CompilerParams(
            collective_id=0, has_side_effects=True, vmem_limit_bytes=60 * 2**20),
    )(tile_rows, tile_cols, tile_count, green_tiles, incident, sources)


def solution(mesh):
    return jax.shard_map(
        functools.partial(shards, mesh.shape["layer"], mesh.shape["tile"]),
        mesh=mesh,
        in_specs=(
            P(None, "tile", None),
            P("layer", None, "tile", None),
            P("layer", "tile", None, None, None),
            P("layer", "tile"),
            P("layer", "tile"),
            P("layer", "tile"),
        ),
        out_specs=P("layer", None, "tile", None),
        check_vma=False,
    )
```

```python
import functools

import jax
import jax.numpy as jnp
from jax import lax
from jax.experimental import pallas as pl
from jax.experimental.pallas import tpu as pltpu
from jax.sharding import PartitionSpec as P

MESH = pl.DeviceIdType.MESH
VMEM = pl.BlockSpec(memory_space=pltpu.VMEM)
HBM = pl.BlockSpec(memory_space=pltpu.HBM)
CHUNKS = 16
LAG = 6
GROUP = 3
F32 = jnp.float32
BF16 = jnp.bfloat16


def sweep(layers, places, rows_hbm, cols_hbm, count_hbm, tiles_hbm, incident_hbm, source_hbm, out_ref,
          rows_ref, cols_ref, count_ref, tiles_ref, incident_ref, source_ref, dense, given, result,
          own_in, ext_in, side_in, mate_in, own_out, ext_out, mate_out, kept,
          index_sem, array_sem, tile_sem,
          own_s, ext_s, side_s, mate_s, own_r, ext_r, side_r, mate_r):
    slots, block = tiles_ref.shape[0], tiles_ref.shape[2]
    chunks, width, rows = own_in.shape
    each, half = chunks // 2, width // 2
    layer, place = lax.axis_index("layer"), lax.axis_index("tile")
    odd = lax.rem(place, 2)
    partner = place + 1 - 2 * odd
    beyond = place - 1 + 2 * odd
    inner = (beyond >= 0) & (beyond < places)
    above, below = layer > 0, layer < layers - 1

    index_copies = [
        pltpu.make_async_copy(src, dst, index_sem.at[i])
        for i, (src, dst) in enumerate(((rows_hbm, rows_ref), (cols_hbm, cols_ref), (count_hbm, count_ref)))
    ]
    array_copies = [
        pltpu.make_async_copy(incident_hbm, incident_ref, array_sem.at[0]),
        pltpu.make_async_copy(source_hbm.at[0], source_ref, array_sem.at[1]),
    ]
    tile_copies = [
        pltpu.make_async_copy(tiles_hbm.at[0, pl.ds(i, GROUP)], tiles_ref.at[pl.ds(i, GROUP)], tile_sem.at[i])
        for i in range(0, slots, GROUP)
    ]
    for copy in index_copies + array_copies[:1] + tile_copies + array_copies[1:]:
        copy.start()

    barrier = pltpu.get_barrier_semaphore()

    def hello(l, t):
        pl.semaphore_signal(barrier, inc=1, device_id=(l, t), device_id_type=MESH)

    hello(layer, partner)

    @pl.when(inner)
    def _():
        hello(layer, beyond)

    @pl.when(above)
    def _():
        hello(layer - 1, place)

    @pl.when(above & inner)
    def _():
        hello(layer - 1, beyond)

    dense[slots] = jnp.zeros(dense.shape[1:], BF16)

    for copy in index_copies:
        copy.wait()
    live = count_ref[0, 0]
    keys = []
    for i in range(slots):
        row = rows_ref[0, i]
        owner = row // 2
        part = jnp.where(owner == beyond, 0, jnp.where(owner == partner, 1, 2))
        keys.append(jnp.where(i < live, part * 4 + (row - 2 * owner) * 2 + cols_ref[0, i], 16 + i))
    before = []
    for i in range(slots):
        found = jnp.int32(slots)
        for j in range(i):
            found = jnp.where(keys[j] == keys[i], j, found)
        before.append(found)
    last = []
    for p in range(12):
        found = jnp.int32(slots)
        for i in range(slots):
            found = jnp.where(keys[i] == p, i, found)
        last.append(found)

    def turn_incident(f):
        @pl.when(jnp.logical_not(above))
        def _():
            turned = incident_ref[f].astype(F32).T.reshape(2, each, half, rows)
            for j in range(each):
                own_in[f * each + j] = turned[:, j].reshape(width, rows).astype(BF16)

    array_copies[0].wait()
    turn_incident(0)

    @pl.when(jnp.logical_not(above & inner))
    def _():
        ext_in[...] = jnp.zeros_like(ext_in)

    @pl.when(jnp.logical_not(inner))
    def _():
        side_in[...] = jnp.zeros_like(ext_in)

    for i in range(slots):
        if i % GROUP == 0:
            tile_copies[i // GROUP].wait()
        for s in range(2):
            dense[i, s] = (tiles_ref[i, s].T.astype(F32) + dense[before[i], s].astype(F32)).astype(BF16)

    def turn_sources():
        array_copies[1].wait()
        turn_incident(1)
        for f in range(2):
            given[f] = source_ref[f].astype(F32).T.reshape(2, each, half, rows)

    pl.semaphore_wait(barrier, (1 + inner.astype(jnp.int32)) * (1 + below.astype(jnp.int32)))

    def send(src, dst, s, r, c, l, t):
        return pltpu.make_async_remote_copy(
            src_ref=src.at[c], dst_ref=dst.at[c], send_sem=s.at[c], recv_sem=r.at[c],
            device_id=(l, t), device_id_type=MESH)

    def to_mate(c):
        return send(mate_out, mate_in, mate_s, mate_r, c, layer, partner)

    def to_side(c):
        return send(ext_out, side_in, side_s, side_r, c, layer, beyond)

    def to_own(c):
        return send(own_out, own_in, own_s, own_r, c, layer + 1, place)

    def to_ext(c):
        return send(ext_out, ext_in, ext_s, ext_r, c, layer + 1, beyond)

    def multiply(c, onward):
        @pl.when(above)
        def _():
            to_own(c).wait_recv()

        @pl.when(above & inner)
        def _():
            to_ext(c).wait_recv()

        u = (own_in[c].astype(F32) + ext_in[c].astype(F32)).astype(BF16).astype(F32)
        sides = (u.astype(BF16), jnp.concatenate([-u[half:], u[:half]], axis=0).astype(BF16))

        def part(k):
            outs = []
            for r in range(2):
                total = None
                for b in range(2):
                    for s in range(2):
                        term = jnp.dot(sides[s][:, b * block:(b + 1) * block],
                                       dense[last[4 * k + 2 * r + b], s], preferred_element_type=F32)
                        total = term if total is None else total + term
                outs.append(total)
            return jnp.concatenate(outs, axis=1)

        def exchange():
            mate_out[c] = part(1).astype(BF16)
            to_mate(c).start()

        if onward:
            exchange()
        ext_out[c] = part(0).astype(BF16)

        @pl.when(inner)
        def _():
            if onward:
                to_ext(c).start()
            to_side(c).start()

        if not onward:
            exchange()
        return lambda: part(2)

    def combine(c, own, onward):
        y = own + mate_in[c].astype(F32) + given[c // each, :, c % each].reshape(width, rows)
        kept[c] = y
        if onward:
            own_out[c] = y.astype(BF16)
            to_own(c).start()

    def finish(c):
        @pl.when(inner)
        def _():
            to_side(c).wait_recv()

        result[c // each, :, c % each] = (kept[c] + side_in[c].astype(F32)).reshape(2, half, rows)

    def pipeline(onward):
        kept[0] = multiply(0, onward)()
        turn_sources()

        def step(t, _):
            own = multiply(t, onward)
            to_mate(t - 1).wait_recv()
            combine(t - 1, kept[t - 1], onward)
            kept[t] = own()

            @pl.when(t >= LAG)
            def _():
                finish(t - LAG)
            return 0

        lax.fori_loop(1, chunks, step, 0)
        to_mate(chunks - 1).wait_recv()
        combine(chunks - 1, kept[chunks - 1], onward)

    @pl.when(below)
    def _():
        pipeline(True)

    @pl.when(jnp.logical_not(below))
    def _():
        pipeline(False)

    def leave(f):
        out_ref[0, f] = result[f].reshape(2 * each * half, rows).T.astype(BF16)

    leave(0)

    def last_step(c, _):
        finish(c)
        return 0

    lax.fori_loop(chunks - LAG, chunks, last_step, 0)
    leave(1)

    def drain(c, _):
        to_mate(c).wait_send()

        @pl.when(inner)
        def _():
            to_side(c).wait_send()

        @pl.when(below)
        def _():
            to_own(c).wait_send()

        @pl.when(below & inner)
        def _():
            to_ext(c).wait_send()
        return 0

    lax.fori_loop(0, chunks, drain, 0)


def shards(layers, places, incident, sources, green_tiles, tile_rows, tile_cols, tile_count):
    fronts, rows, columns = incident.shape
    slots, _, block, _ = green_tiles.shape[1:]
    width = fronts * columns // CHUNKS
    buffer = pltpu.VMEM((CHUNKS, width, rows), BF16)
    split = pltpu.VMEM((fronts, 2, CHUNKS // 2, width // 2, rows), F32)
    return pl.pallas_call(
        functools.partial(sweep, layers, places),
        out_shape=pltpu.VMEM((1, fronts, rows, columns), BF16),
        in_specs=[HBM] * 6,
        out_specs=VMEM,
        scratch_shapes=[
            pltpu.SMEM(tile_rows.shape, jnp.int32),
            pltpu.SMEM(tile_cols.shape, jnp.int32),
            pltpu.SMEM(tile_count.shape, jnp.int32),
            pltpu.VMEM((slots, 2, block, block), BF16),
            pltpu.VMEM((fronts, rows, columns), BF16),
            pltpu.VMEM((fronts, rows, columns), BF16),
            pltpu.VMEM((slots + 1, 2, block, block), BF16),
            split,
            split,
        ]
        + [buffer] * 7
        + [pltpu.VMEM((CHUNKS, width, rows), F32)]
        + [pltpu.SemaphoreType.DMA((3,)), pltpu.SemaphoreType.DMA((2,)), pltpu.SemaphoreType.DMA((slots,))]
        + [pltpu.SemaphoreType.DMA((CHUNKS,))] * 8,
        compiler_params=pltpu.CompilerParams(
            collective_id=0, has_side_effects=True, vmem_limit_bytes=32 * 2**20),
    )(
        pltpu.with_memory_space_constraint(tile_rows, pltpu.HBM),
        pltpu.with_memory_space_constraint(tile_cols, pltpu.HBM),
        tile_count,
        pltpu.with_memory_space_constraint(green_tiles, pltpu.HBM),
        pltpu.with_memory_space_constraint(incident, pltpu.HBM),
        pltpu.with_memory_space_constraint(sources, pltpu.HBM),
    )


def solution(mesh):
    return jax.shard_map(
        functools.partial(shards, mesh.shape["layer"], mesh.shape["tile"]),
        mesh=mesh,
        in_specs=(
            P(None, "tile", None),
            P("layer", None, "tile", None),
            P("layer", "tile", None, None, None),
            P("layer", "tile"),
            P("layer", "tile"),
            P("layer", "tile"),
        ),
        out_specs=P("layer", None, "tile", None),
        check_vma=False,
    )
```

```python
import functools

import jax
import jax.numpy as jnp
from jax import lax
from jax.experimental import pallas as pl
from jax.experimental.pallas import tpu as pltpu
from jax.sharding import PartitionSpec as P

MESH = pl.DeviceIdType.MESH
VMEM = pl.BlockSpec(memory_space=pltpu.VMEM)
HBM = pl.BlockSpec(memory_space=pltpu.HBM)
CHUNKS = 16
LAG = 6
GROUP = 3
ROW = 16
F32 = jnp.float32
BF16 = jnp.bfloat16


def sweep(layers, places, rows_hbm, cols_hbm, count_hbm, tiles_hbm, incident_hbm, source_hbm, out_ref,
          rows_ref, cols_ref, count_ref, tiles_ref, incident_ref, source_ref, dense, given, result,
          own_in, ext_in, side_in, mate_in, own_out, ext_out, mate_out, kept,
          index_sem, array_sem, tile_sem,
          own_s, ext_s, side_s, mate_s, own_r, ext_r, side_r, mate_r):
    slots, block = tiles_ref.shape[0], tiles_ref.shape[2]
    chunks, width, rows = own_in.shape
    each, half = chunks // 2, width // 2
    layer, place = lax.axis_index("layer"), lax.axis_index("tile")
    odd = lax.rem(place, 2)
    partner = place + 1 - 2 * odd
    beyond = place - 1 + 2 * odd
    inner = (beyond >= 0) & (beyond < places)
    outer = jnp.logical_not(inner)
    far = inner & ((lax.rem(place, ROW) == 0) | (lax.rem(place, ROW) == ROW - 1))
    above, below = layer > 0, layer < layers - 1

    index_copies = [
        pltpu.make_async_copy(src, dst, index_sem.at[i])
        for i, (src, dst) in enumerate(((rows_hbm, rows_ref), (cols_hbm, cols_ref), (count_hbm, count_ref)))
    ]
    array_copies = [
        pltpu.make_async_copy(incident_hbm, incident_ref, array_sem.at[0]),
        pltpu.make_async_copy(source_hbm.at[0], source_ref, array_sem.at[1]),
    ]
    tile_copies = [
        pltpu.make_async_copy(tiles_hbm.at[0, pl.ds(i, GROUP)], tiles_ref.at[pl.ds(i, GROUP)], tile_sem.at[i])
        for i in range(0, slots, GROUP)
    ]
    for copy in index_copies + array_copies[:1] + tile_copies + array_copies[1:]:
        copy.start()

    barrier = pltpu.get_barrier_semaphore()

    def hello(l, t):
        pl.semaphore_signal(barrier, inc=1, device_id=(l, t), device_id_type=MESH)

    hello(layer, partner)

    @pl.when(inner)
    def _():
        hello(layer, beyond)

    @pl.when(above)
    def _():
        hello(layer - 1, place)

    @pl.when(above & inner)
    def _():
        hello(layer - 1, beyond)

    dense[slots] = jnp.zeros(dense.shape[1:], BF16)

    for copy in index_copies:
        copy.wait()
    live = count_ref[0, 0]
    keys = []
    for i in range(slots):
        row = rows_ref[0, i]
        owner = row // 2
        part = jnp.where(owner == beyond, 0, jnp.where(owner == partner, 1, 2))
        keys.append(jnp.where(i < live, part * 4 + (row - 2 * owner) * 2 + cols_ref[0, i], 16 + i))
    before = []
    for i in range(slots):
        found = jnp.int32(slots)
        for j in range(i):
            found = jnp.where(keys[j] == keys[i], j, found)
        before.append(found)
    last = []
    for p in range(12):
        found = jnp.int32(slots)
        for i in range(slots):
            found = jnp.where(keys[i] == p, i, found)
        last.append(found)

    def turn_incident(f):
        @pl.when(jnp.logical_not(above))
        def _():
            turned = incident_ref[f].astype(F32).T.reshape(2, each, half, rows)
            for j in range(each):
                own_in[f * each + j] = turned[:, j].reshape(width, rows).astype(BF16)

    array_copies[0].wait()
    turn_incident(0)

    @pl.when(jnp.logical_not(above & inner))
    def _():
        ext_in[...] = jnp.zeros_like(ext_in)

    for i in range(slots):
        if i % GROUP == 0:
            tile_copies[i // GROUP].wait()
        for s in range(2):
            dense[i, s] = (tiles_ref[i, s].T.astype(F32) + dense[before[i], s].astype(F32)).astype(BF16)

    def turn_sources():
        array_copies[1].wait()
        turn_incident(1)
        for f in range(2):
            given[f] = source_ref[f].astype(F32).T.reshape(2, each, half, rows)

    pl.semaphore_wait(barrier, (1 + inner.astype(jnp.int32)) * (1 + below.astype(jnp.int32)))

    def send(src, dst, s, r, c, l, t):
        return pltpu.make_async_remote_copy(
            src_ref=src.at[c], dst_ref=dst.at[c], send_sem=s.at[c], recv_sem=r.at[c],
            device_id=(l, t), device_id_type=MESH)

    def to_mate(c):
        return send(mate_out, mate_in, mate_s, mate_r, c, layer, partner)

    def to_side(c):
        return send(ext_out, side_in, side_s, side_r, c, layer, beyond)

    def to_own(c):
        return send(own_out, own_in, own_s, own_r, c, layer + 1, place)

    def to_ext(c):
        return send(ext_out, ext_in, ext_s, ext_r, c, layer + 1, beyond)

    def multiply(c, onward, kind):
        @pl.when(above)
        def _():
            to_own(c).wait_recv()
            if kind != "outer":
                to_ext(c).wait_recv()

        u = (own_in[c].astype(F32) + ext_in[c].astype(F32)).astype(BF16).astype(F32)
        sides = (u.astype(BF16), jnp.concatenate([-u[half:], u[:half]], axis=0).astype(BF16))

        def part(k):
            outs = []
            for r in range(2):
                total = None
                for b in range(2):
                    for s in range(2):
                        term = jnp.dot(sides[s][:, b * block:(b + 1) * block],
                                       dense[last[4 * k + 2 * r + b], s], preferred_element_type=F32)
                        total = term if total is None else total + term
                outs.append(total)
            return jnp.concatenate(outs, axis=1)

        def exchange():
            mate_out[c] = part(1).astype(BF16)
            to_mate(c).start()

        def reach():
            ext_out[c] = part(0).astype(BF16)
            if onward:
                to_ext(c).start()
            to_side(c).start()

        if kind == "far":
            reach()
            exchange()
        else:
            exchange()
            if kind != "outer":
                reach()
        return lambda: part(2)

    def combine(c, own, kind, onward):
        y = own + given[c // each, :, c % each].reshape(width, rows) + mate_in[c].astype(F32)
        if kind == "outer":
            result[c // each, :, c % each] = y.reshape(2, half, rows)
        else:
            kept[c] = y
        if onward:
            own_out[c] = y.astype(BF16)
            to_own(c).start()

    def finish(c):
        to_side(c).wait_recv()
        result[c // each, :, c % each] = (kept[c] + side_in[c].astype(F32)).reshape(2, half, rows)

    def pipeline(onward, kind):
        kept[0] = multiply(0, onward, kind)()
        turn_sources()

        def step(t, _):
            own = multiply(t, onward, kind)
            to_mate(t - 1).wait_recv()
            combine(t - 1, kept[t - 1], kind, onward)
            kept[t] = own()
            if kind != "outer":
                @pl.when(t >= LAG)
                def _():
                    finish(t - LAG)
            return 0

        lax.fori_loop(1, chunks, step, 0)
        to_mate(chunks - 1).wait_recv()
        combine(chunks - 1, kept[chunks - 1], kind, onward)
        leave(0)

        def last_step(c, _):
            finish(c)
            return 0

        if kind != "outer":
            lax.fori_loop(chunks - LAG, chunks, last_step, 0)

    def leave(f):
        out_ref[0, f] = result[f].reshape(2 * each * half, rows).T.astype(BF16)

    plain = jnp.logical_not(far | outer)
    for onward, mine in ((True, below), (False, jnp.logical_not(below))):
        for kind, such in (("plain", plain), ("far", far), ("outer", outer)):
            if onward or kind in ("far", "outer"):
                if not onward and kind == "far":
                    such = inner

                @pl.when(mine & such)
                def _():
                    pipeline(onward, kind)

    leave(1)

    def drain(c, _):
        to_mate(c).wait_send()

        @pl.when(inner)
        def _():
            to_side(c).wait_send()

        @pl.when(below)
        def _():
            to_own(c).wait_send()

        @pl.when(below & inner)
        def _():
            to_ext(c).wait_send()
        return 0

    lax.fori_loop(0, chunks, drain, 0)


def shards(layers, places, incident, sources, green_tiles, tile_rows, tile_cols, tile_count):
    fronts, rows, columns = incident.shape
    slots, _, block, _ = green_tiles.shape[1:]
    width = fronts * columns // CHUNKS
    buffer = pltpu.VMEM((CHUNKS, width, rows), BF16)
    split = pltpu.VMEM((fronts, 2, CHUNKS // 2, width // 2, rows), F32)
    return pl.pallas_call(
        functools.partial(sweep, layers, places),
        out_shape=pltpu.VMEM((1, fronts, rows, columns), BF16),
        in_specs=[HBM] * 6,
        out_specs=VMEM,
        scratch_shapes=[
            pltpu.SMEM(tile_rows.shape, jnp.int32),
            pltpu.SMEM(tile_cols.shape, jnp.int32),
            pltpu.SMEM(tile_count.shape, jnp.int32),
            pltpu.VMEM((slots, 2, block, block), BF16),
            pltpu.VMEM((fronts, rows, columns), BF16),
            pltpu.VMEM((fronts, rows, columns), BF16),
            pltpu.VMEM((slots + 1, 2, block, block), BF16),
            split,
            split,
        ]
        + [buffer] * 7
        + [pltpu.VMEM((CHUNKS, width, rows), F32)]
        + [pltpu.SemaphoreType.DMA((3,)), pltpu.SemaphoreType.DMA((2,)), pltpu.SemaphoreType.DMA((slots,))]
        + [pltpu.SemaphoreType.DMA((CHUNKS,))] * 8,
        compiler_params=pltpu.CompilerParams(
            collective_id=0, has_side_effects=True, vmem_limit_bytes=32 * 2**20),
    )(
        pltpu.with_memory_space_constraint(tile_rows, pltpu.HBM),
        pltpu.with_memory_space_constraint(tile_cols, pltpu.HBM),
        tile_count,
        pltpu.with_memory_space_constraint(green_tiles, pltpu.HBM),
        pltpu.with_memory_space_constraint(incident, pltpu.HBM),
        pltpu.with_memory_space_constraint(sources, pltpu.HBM),
    )


def solution(mesh):
    return jax.shard_map(
        functools.partial(shards, mesh.shape["layer"], mesh.shape["tile"]),
        mesh=mesh,
        in_specs=(
            P(None, "tile", None),
            P("layer", None, "tile", None),
            P("layer", "tile", None, None, None),
            P("layer", "tile"),
            P("layer", "tile"),
            P("layer", "tile"),
        ),
        out_specs=P("layer", None, "tile", None),
        check_vma=False,
    )
```

```python
import functools

import jax
import jax.numpy as jnp
from jax import lax
from jax.experimental import pallas as pl
from jax.experimental.pallas import tpu as pltpu
from jax.sharding import PartitionSpec as P

MESH = pl.DeviceIdType.MESH
VMEM = pl.BlockSpec(memory_space=pltpu.VMEM)
HBM = pl.BlockSpec(memory_space=pltpu.HBM)
CHUNKS = 16
LAG = 6
GROUP = 3
ROW = 16
F32 = jnp.float32
BF16 = jnp.bfloat16


def sweep(layers, places, rows_hbm, cols_hbm, count_hbm, tiles_hbm, incident_hbm, source_hbm, out_ref,
          rows_ref, cols_ref, count_ref, tiles_ref, incident_ref, source_ref, dense, given, result,
          own_in, ext_in, side_in, mate_in, own_out, ext_out, mate_out, kept,
          index_sem, array_sem, tile_sem,
          own_s, ext_s, side_s, mate_s, own_r, ext_r, side_r, mate_r):
    slots, block = tiles_ref.shape[0], tiles_ref.shape[2]
    chunks, width, rows = own_in.shape
    each, half = chunks // 2, width // 2
    layer, place = lax.axis_index("layer"), lax.axis_index("tile")
    odd = lax.rem(place, 2)
    partner = place + 1 - 2 * odd
    beyond = place - 1 + 2 * odd
    inner = (beyond >= 0) & (beyond < places)
    outer = jnp.logical_not(inner)
    far = inner & ((lax.rem(place, ROW) == 0) | (lax.rem(place, ROW) == ROW - 1))
    above, below = layer > 0, layer < layers - 1

    index_copies = [
        pltpu.make_async_copy(src, dst, index_sem.at[i])
        for i, (src, dst) in enumerate(((rows_hbm, rows_ref), (cols_hbm, cols_ref), (count_hbm, count_ref)))
    ]
    array_copies = [
        pltpu.make_async_copy(incident_hbm, incident_ref, array_sem.at[0]),
        pltpu.make_async_copy(source_hbm.at[0], source_ref, array_sem.at[1]),
    ]
    tile_copies = [
        pltpu.make_async_copy(tiles_hbm.at[0, pl.ds(i, GROUP)], tiles_ref.at[pl.ds(i, GROUP)], tile_sem.at[i])
        for i in range(0, slots, GROUP)
    ]
    barrier = pltpu.get_barrier_semaphore()

    def hello(l, t):
        pl.semaphore_signal(barrier, inc=1, device_id=(l, t), device_id_type=MESH)

    hello(layer, partner)

    @pl.when(inner)
    def _():
        hello(layer, beyond)

    @pl.when(above)
    def _():
        hello(layer - 1, place)

    @pl.when(above & inner)
    def _():
        hello(layer - 1, beyond)

    for copy in index_copies + array_copies[:1] + tile_copies + array_copies[1:]:
        copy.start()

    dense[slots] = jnp.zeros(dense.shape[1:], BF16)

    for copy in index_copies:
        copy.wait()
    live = count_ref[0, 0]
    keys = []
    for i in range(slots):
        row = rows_ref[0, i]
        owner = row // 2
        part = jnp.where(owner == beyond, 0, jnp.where(owner == partner, 1, 2))
        keys.append(jnp.where(i < live, part * 4 + (row - 2 * owner) * 2 + cols_ref[0, i], 16 + i))
    before = []
    for i in range(slots):
        found = jnp.int32(slots)
        for j in range(i):
            found = jnp.where(keys[j] == keys[i], j, found)
        before.append(found)
    last = []
    for p in range(12):
        found = jnp.int32(slots)
        for i in range(slots):
            found = jnp.where(keys[i] == p, i, found)
        last.append(found)

    def turn_incident(f):
        @pl.when(jnp.logical_not(above))
        def _():
            turned = incident_ref[f].astype(F32).T.reshape(2, each, half, rows)
            for j in range(each):
                own_in[f * each + j] = turned[:, j].reshape(width, rows).astype(BF16)

    array_copies[0].wait()
    turn_incident(0)

    @pl.when(jnp.logical_not(above & inner))
    def _():
        ext_in[...] = jnp.zeros_like(ext_in)

    for i in range(slots):
        if i % GROUP == 0:
            tile_copies[i // GROUP].wait()
        for s in range(2):
            dense[i, s] = (tiles_ref[i, s].T.astype(F32) + dense[before[i], s].astype(F32)).astype(BF16)

    def turn_sources():
        array_copies[1].wait()
        turn_incident(1)
        for f in range(2):
            given[f] = source_ref[f].astype(F32).T.reshape(2, each, half, rows)

    pl.semaphore_wait(barrier, (1 + inner.astype(jnp.int32)) * (1 + below.astype(jnp.int32)))

    def send(src, dst, s, r, c, l, t):
        return pltpu.make_async_remote_copy(
            src_ref=src.at[c], dst_ref=dst.at[c], send_sem=s.at[c], recv_sem=r.at[c],
            device_id=(l, t), device_id_type=MESH)

    def to_mate(c):
        return send(mate_out, mate_in, mate_s, mate_r, c, layer, partner)

    def to_side(c):
        return send(ext_out, side_in, side_s, side_r, c, layer, beyond)

    def to_own(c):
        return send(own_out, own_in, own_s, own_r, c, layer + 1, place)

    def to_ext(c):
        return send(ext_out, ext_in, ext_s, ext_r, c, layer + 1, beyond)

    def multiply(c, onward, kind):
        @pl.when(above)
        def _():
            to_own(c).wait_recv()
            if kind != "outer":
                to_ext(c).wait_recv()

        u = (own_in[c].astype(F32) + ext_in[c].astype(F32)).astype(BF16).astype(F32)
        sides = (u.astype(BF16), jnp.concatenate([-u[half:], u[:half]], axis=0).astype(BF16))

        def part(k):
            outs = []
            for r in range(2):
                total = None
                for b in range(2):
                    for s in range(2):
                        term = jnp.dot(sides[s][:, b * block:(b + 1) * block],
                                       dense[last[4 * k + 2 * r + b], s], preferred_element_type=F32)
                        total = term if total is None else total + term
                outs.append(total)
            return jnp.concatenate(outs, axis=1)

        def exchange():
            mate_out[c] = part(1).astype(BF16)
            to_mate(c).start()

        def reach():
            ext_out[c] = part(0).astype(BF16)
            if onward:
                to_ext(c).start()
            to_side(c).start()

        if kind == "far":
            reach()
            exchange()
        else:
            exchange()
            if kind != "outer":
                reach()
        return lambda: part(2)

    def combine(c, own, kind, onward):
        y = own + given[c // each, :, c % each].reshape(width, rows) + mate_in[c].astype(F32)
        if kind == "outer":
            result[c // each, :, c % each] = y.reshape(2, half, rows)
        else:
            kept[c] = y
        if onward:
            own_out[c] = y.astype(BF16)
            to_own(c).start()

    def finish(c):
        to_side(c).wait_recv()
        result[c // each, :, c % each] = (kept[c] + side_in[c].astype(F32)).reshape(2, half, rows)

    def pipeline(onward, kind):
        kept[0] = multiply(0, onward, kind)()
        turn_sources()

        def step(t, _):
            own = multiply(t, onward, kind)
            to_mate(t - 1).wait_recv()
            combine(t - 1, kept[t - 1], kind, onward)
            kept[t] = own()
            if kind != "outer":
                @pl.when(t >= LAG)
                def _():
                    finish(t - LAG)
            return 0

        lax.fori_loop(1, chunks, step, 0)
        to_mate(chunks - 1).wait_recv()
        combine(chunks - 1, kept[chunks - 1], kind, onward)
        leave(0)

        def last_step(c, _):
            finish(c)
            return 0

        if kind != "outer":
            lax.fori_loop(chunks - LAG, chunks, last_step, 0)

    def leave(f):
        out_ref[0, f] = result[f].reshape(2 * each * half, rows).T.astype(BF16)

    plain = jnp.logical_not(far | outer)
    for onward, mine in ((True, below), (False, jnp.logical_not(below))):
        for kind, such in (("plain", plain), ("far", far), ("outer", outer)):
            if onward or kind in ("far", "outer"):
                if not onward and kind == "far":
                    such = inner

                @pl.when(mine & such)
                def _():
                    pipeline(onward, kind)

    leave(1)

    def drain(c, _):
        to_mate(c).wait_send()

        @pl.when(inner)
        def _():
            to_side(c).wait_send()

        @pl.when(below)
        def _():
            to_own(c).wait_send()

        @pl.when(below & inner)
        def _():
            to_ext(c).wait_send()
        return 0

    lax.fori_loop(0, chunks, drain, 0)


def shards(layers, places, incident, sources, green_tiles, tile_rows, tile_cols, tile_count):
    fronts, rows, columns = incident.shape
    slots, _, block, _ = green_tiles.shape[1:]
    width = fronts * columns // CHUNKS
    buffer = pltpu.VMEM((CHUNKS, width, rows), BF16)
    split = pltpu.VMEM((fronts, 2, CHUNKS // 2, width // 2, rows), F32)
    return pl.pallas_call(
        functools.partial(sweep, layers, places),
        out_shape=pltpu.VMEM((1, fronts, rows, columns), BF16),
        in_specs=[HBM] * 6,
        out_specs=VMEM,
        scratch_shapes=[
            pltpu.SMEM(tile_rows.shape, jnp.int32),
            pltpu.SMEM(tile_cols.shape, jnp.int32),
            pltpu.SMEM(tile_count.shape, jnp.int32),
            pltpu.VMEM((slots, 2, block, block), BF16),
            pltpu.VMEM((fronts, rows, columns), BF16),
            pltpu.VMEM((fronts, rows, columns), BF16),
            pltpu.VMEM((slots + 1, 2, block, block), BF16),
            split,
            split,
        ]
        + [buffer] * 7
        + [pltpu.VMEM((CHUNKS, width, rows), F32)]
        + [pltpu.SemaphoreType.DMA((3,)), pltpu.SemaphoreType.DMA((2,)), pltpu.SemaphoreType.DMA((slots,))]
        + [pltpu.SemaphoreType.DMA((CHUNKS,))] * 8,
        compiler_params=pltpu.CompilerParams(
            collective_id=0, has_side_effects=True, vmem_limit_bytes=32 * 2**20),
    )(
        pltpu.with_memory_space_constraint(tile_rows, pltpu.HBM),
        pltpu.with_memory_space_constraint(tile_cols, pltpu.HBM),
        tile_count,
        pltpu.with_memory_space_constraint(green_tiles, pltpu.HBM),
        pltpu.with_memory_space_constraint(incident, pltpu.HBM),
        pltpu.with_memory_space_constraint(sources, pltpu.HBM),
    )


def solution(mesh):
    return jax.shard_map(
        functools.partial(shards, mesh.shape["layer"], mesh.shape["tile"]),
        mesh=mesh,
        in_specs=(
            P(None, "tile", None),
            P("layer", None, "tile", None),
            P("layer", "tile", None, None, None),
            P("layer", "tile"),
            P("layer", "tile"),
            P("layer", "tile"),
        ),
        out_specs=P("layer", None, "tile", None),
        check_vma=False,
    )
```

```python
import functools

import jax
import jax.numpy as jnp
from jax import lax
from jax.experimental import pallas as pl
from jax.experimental.pallas import tpu as pltpu
from jax.sharding import PartitionSpec as P

MESH = pl.DeviceIdType.MESH
VMEM = pl.BlockSpec(memory_space=pltpu.VMEM)
HBM = pl.BlockSpec(memory_space=pltpu.HBM)
CHUNKS = 16
LAG = 6
GROUP = 3
ROW = 16
F32 = jnp.float32
BF16 = jnp.bfloat16


def sweep(layers, places, rows_hbm, cols_hbm, count_hbm, tiles_hbm, incident_hbm, source_hbm, out_ref,
          rows_ref, cols_ref, count_ref, tiles_ref, incident_ref, source_ref, dense, given, result,
          own_in, ext_in, side_in, mate_in, own_out, ext_out, mate_out, kept,
          index_sem, array_sem, tile_sem,
          own_s, ext_s, side_s, mate_s, own_r, ext_r, side_r, mate_r):
    slots, block = tiles_ref.shape[0], tiles_ref.shape[2]
    chunks, width, rows = own_in.shape
    each, half = chunks // 2, width // 2
    layer, place = lax.axis_index("layer"), lax.axis_index("tile")
    odd = lax.rem(place, 2)
    partner = place + 1 - 2 * odd
    beyond = place - 1 + 2 * odd
    inner = (beyond >= 0) & (beyond < places)
    outer = jnp.logical_not(inner)
    far = inner & ((lax.rem(place, ROW) == 0) | (lax.rem(place, ROW) == ROW - 1))
    above, below = layer > 0, layer < layers - 1

    index_copies = [
        pltpu.make_async_copy(src, dst, index_sem.at[i])
        for i, (src, dst) in enumerate(((rows_hbm, rows_ref), (cols_hbm, cols_ref), (count_hbm, count_ref)))
    ]
    array_copies = [
        pltpu.make_async_copy(incident_hbm, incident_ref, array_sem.at[0]),
        pltpu.make_async_copy(source_hbm.at[0], source_ref, array_sem.at[1]),
    ]
    tile_copies = [
        pltpu.make_async_copy(tiles_hbm.at[0, pl.ds(i, GROUP)], tiles_ref.at[pl.ds(i, GROUP)], tile_sem.at[i])
        for i in range(0, slots, GROUP)
    ]
    barrier = pltpu.get_barrier_semaphore()

    def hello(l, t):
        pl.semaphore_signal(barrier, inc=1, device_id=(l, t), device_id_type=MESH)

    hello(layer, partner)

    @pl.when(inner)
    def _():
        hello(layer, beyond)

    @pl.when(above)
    def _():
        hello(layer - 1, place)

    @pl.when(above & inner)
    def _():
        hello(layer - 1, beyond)

    for copy in index_copies + array_copies[:1] + tile_copies + array_copies[1:]:
        copy.start()

    dense[slots] = jnp.zeros(dense.shape[1:], BF16)

    for copy in index_copies:
        copy.wait()
    live = count_ref[0, 0]
    keys = []
    for i in range(slots):
        row = rows_ref[0, i]
        owner = row // 2
        part = jnp.where(owner == beyond, 0, jnp.where(owner == partner, 1, 2))
        keys.append(jnp.where(i < live, part * 4 + (row - 2 * owner) * 2 + cols_ref[0, i], 16 + i))
    before = []
    for i in range(slots):
        found = jnp.int32(slots)
        for j in range(i):
            found = jnp.where(keys[j] == keys[i], j, found)
        before.append(found)
    last = []
    for p in range(12):
        found = jnp.int32(slots)
        for i in range(slots):
            found = jnp.where(keys[i] == p, i, found)
        last.append(found)

    def turn_incident(f):
        @pl.when(jnp.logical_not(above))
        def _():
            turned = incident_ref[f].astype(F32).T.reshape(2, each, half, rows)
            for j in range(each):
                own_in[f * each + j] = turned[:, j].reshape(width, rows).astype(BF16)

    array_copies[0].wait()
    turn_incident(0)

    @pl.when(jnp.logical_not(above & inner))
    def _():
        ext_in[...] = jnp.zeros_like(ext_in)

    for i in range(slots):
        if i % GROUP == 0:
            tile_copies[i // GROUP].wait()
        for s in range(2):
            dense[i, s] = (tiles_ref[i, s].T.astype(F32) + dense[before[i], s].astype(F32)).astype(BF16)

    def turn_sources():
        array_copies[1].wait()
        turn_incident(1)
        for f in range(2):
            given[f] = source_ref[f].astype(F32).T.reshape(2, each, half, rows)

    pl.semaphore_wait(barrier, (1 + inner.astype(jnp.int32)) * (1 + below.astype(jnp.int32)))

    def send(src, dst, s, r, c, l, t):
        return pltpu.make_async_remote_copy(
            src_ref=src.at[c], dst_ref=dst.at[c], send_sem=s.at[c], recv_sem=r.at[c],
            device_id=(l, t), device_id_type=MESH)

    def to_mate(c):
        return send(mate_out, mate_in, mate_s, mate_r, c, layer, partner)

    def to_side(c):
        return send(ext_out, side_in, side_s, side_r, c, layer, beyond)

    def to_own(c):
        return send(own_out, own_in, own_s, own_r, c, layer + 1, place)

    def to_ext(c):
        return send(ext_out, ext_in, ext_s, ext_r, c, layer + 1, beyond)

    def depart(c, onward):
        if onward:
            to_ext(c).start()
        to_side(c).start()

    def multiply(c, onward, kind):
        @pl.when(above)
        def _():
            to_own(c).wait_recv()
            if kind != "outer":
                to_ext(c).wait_recv()

        u = (own_in[c].astype(F32) + ext_in[c].astype(F32)).astype(BF16).astype(F32)
        sides = (u.astype(BF16), jnp.concatenate([-u[half:], u[:half]], axis=0).astype(BF16))

        def part(k):
            outs = []
            for r in range(2):
                total = None
                for b in range(2):
                    for s in range(2):
                        term = jnp.dot(sides[s][:, b * block:(b + 1) * block],
                                       dense[last[4 * k + 2 * r + b], s], preferred_element_type=F32)
                        total = term if total is None else total + term
                outs.append(total)
            return jnp.concatenate(outs, axis=1)

        def exchange():
            mate_out[c] = part(1).astype(BF16)
            to_mate(c).start()

        def reach():
            ext_out[c] = part(0).astype(BF16)
            if kind != "plain":
                depart(c, onward)

        if kind == "far":
            reach()
            exchange()
        else:
            exchange()
            if kind != "outer":
                reach()
        return lambda: part(2)

    def combine(c, own, kind, onward):
        y = own + given[c // each, :, c % each].reshape(width, rows) + mate_in[c].astype(F32)
        if kind == "outer":
            result[c // each, :, c % each] = y.reshape(2, half, rows)
        else:
            kept[c] = y
        if onward:
            own_out[c] = y.astype(BF16)
            to_own(c).start()

    def finish(c):
        to_side(c).wait_recv()
        result[c // each, :, c % each] = (kept[c] + side_in[c].astype(F32)).reshape(2, half, rows)

    def pipeline(onward, kind):
        own = multiply(0, onward, kind)
        if kind == "plain":
            depart(0, onward)
        kept[0] = own()
        turn_sources()

        def step(t, _):
            own = multiply(t, onward, kind)
            to_mate(t - 1).wait_recv()
            combine(t - 1, kept[t - 1], kind, onward)
            if kind == "plain":
                depart(t, onward)
            kept[t] = own()
            if kind != "outer":
                @pl.when(t >= LAG)
                def _():
                    finish(t - LAG)
            return 0

        lax.fori_loop(1, chunks, step, 0)
        to_mate(chunks - 1).wait_recv()
        combine(chunks - 1, kept[chunks - 1], kind, onward)
        leave(0)

        def last_step(c, _):
            finish(c)
            return 0

        if kind != "outer":
            lax.fori_loop(chunks - LAG, chunks, last_step, 0)

    def leave(f):
        out_ref[0, f] = result[f].reshape(2 * each * half, rows).T.astype(BF16)

    plain = jnp.logical_not(far | outer)
    for onward, mine in ((True, below), (False, jnp.logical_not(below))):
        for kind, such in (("plain", plain), ("far", far), ("outer", outer)):
            if onward or kind in ("far", "outer"):
                if not onward and kind == "far":
                    such = inner

                @pl.when(mine & such)
                def _():
                    pipeline(onward, kind)

    leave(1)

    def drain(c, _):
        to_mate(c).wait_send()

        @pl.when(inner)
        def _():
            to_side(c).wait_send()

        @pl.when(below)
        def _():
            to_own(c).wait_send()

        @pl.when(below & inner)
        def _():
            to_ext(c).wait_send()
        return 0

    lax.fori_loop(0, chunks, drain, 0)


def shards(layers, places, incident, sources, green_tiles, tile_rows, tile_cols, tile_count):
    fronts, rows, columns = incident.shape
    slots, _, block, _ = green_tiles.shape[1:]
    width = fronts * columns // CHUNKS
    buffer = pltpu.VMEM((CHUNKS, width, rows), BF16)
    split = pltpu.VMEM((fronts, 2, CHUNKS // 2, width // 2, rows), F32)
    return pl.pallas_call(
        functools.partial(sweep, layers, places),
        out_shape=pltpu.VMEM((1, fronts, rows, columns), BF16),
        in_specs=[HBM] * 6,
        out_specs=VMEM,
        scratch_shapes=[
            pltpu.SMEM(tile_rows.shape, jnp.int32),
            pltpu.SMEM(tile_cols.shape, jnp.int32),
            pltpu.SMEM(tile_count.shape, jnp.int32),
            pltpu.VMEM((slots, 2, block, block), BF16),
            pltpu.VMEM((fronts, rows, columns), BF16),
            pltpu.VMEM((fronts, rows, columns), BF16),
            pltpu.VMEM((slots + 1, 2, block, block), BF16),
            split,
            split,
        ]
        + [buffer] * 7
        + [pltpu.VMEM((CHUNKS, width, rows), F32)]
        + [pltpu.SemaphoreType.DMA((3,)), pltpu.SemaphoreType.DMA((2,)), pltpu.SemaphoreType.DMA((slots,))]
        + [pltpu.SemaphoreType.DMA((CHUNKS,))] * 8,
        compiler_params=pltpu.CompilerParams(
            collective_id=0, has_side_effects=True, vmem_limit_bytes=32 * 2**20),
    )(
        pltpu.with_memory_space_constraint(tile_rows, pltpu.HBM),
        pltpu.with_memory_space_constraint(tile_cols, pltpu.HBM),
        tile_count,
        pltpu.with_memory_space_constraint(green_tiles, pltpu.HBM),
        pltpu.with_memory_space_constraint(incident, pltpu.HBM),
        pltpu.with_memory_space_constraint(sources, pltpu.HBM),
    )


def solution(mesh):
    return jax.shard_map(
        functools.partial(shards, mesh.shape["layer"], mesh.shape["tile"]),
        mesh=mesh,
        in_specs=(
            P(None, "tile", None),
            P("layer", None, "tile", None),
            P("layer", "tile", None, None, None),
            P("layer", "tile"),
            P("layer", "tile"),
            P("layer", "tile"),
        ),
        out_specs=P("layer", None, "tile", None),
        check_vma=False,
    )
```
